32 devices in a mesh: parts: 2 (over x), blk: 8 (over z, y), section: 2 (over core).
Axes of the slice: x: 2, y: 2, z: 4, core: 2. Of those that a mesh axis runs over, the one named last changes fastest.
Arguments:
- points: float32 [8, 16384], P(None, ('parts', 'blk')), parts along dimension 1, may hold values from -6 to 6
- rhs: float32 [8, 16384], P(None, ('parts', 'blk')), parts along dimension 1, may hold values from -6 to 6
- scales: float32 [16], P('parts'), parts along dimension 0, may hold values from 1 to 4
Outputs:
- product: float32 [8, 16384], P(None, ('parts', 'blk')), parts along dimension 1
The draws below stay inside these ranges and needn't reach their ends.
There are 2 independent parts, one for each index of `parts`. The reference program is written for one: setup_inputs(seed, part) draws one part's arguments, and reference() takes and returns one part's arrays. A program takes and returns all parts, laid end to end along the dimension named above; each array names one. Nothing has to cross between parts.
All inputs are finite; a program needn't handle non-finite values.
Results may differ from the reference program's by a relative error of at most 0.00009.
Values sent between devices are 32-bit elements; how exact they have to be, the bound alone decides.
No kernel may reach another device: no remote copies, remote signals or barrier semaphores. Data moves between devices by JAX's collectives and lax.ppermute only.
A program may use at most 64 MiB of HBM per device.

```python
import math
import jax
import jax.numpy as jnp
from jax import lax

F = 8
R = 8
B = 1024
BLOCKS = 8
N = 8192


def levels(stream_key, extent, cuts, smallest, largest):
    factor_of = 1.0
    for dim, blocks in cuts:
        draws = jax.random.uniform(jax.random.fold_in(jax.random.fold_in(stream_key, 6), dim), (blocks,), jnp.float32, smallest / len(cuts), largest / len(cuts))
        factor_of = factor_of * jnp.repeat(jnp.exp(draws), extent[dim] // blocks).reshape((-1,) + (1,) * (len(extent) - 1 - dim))
    return factor_of


def normal_values(own_key, dims, deviation, bound, cuts=(), held_as=jnp.bfloat16):
    level = levels(own_key, dims, cuts, -0.22, 0.18) if cuts else 1.0
    values = jax.random.normal(own_key, dims, jnp.float32) * deviation * level
    return jnp.minimum(jnp.maximum(values, -bound), bound).astype(held_as)


def setup_inputs(seed: int = 0, part: int = 0) -> dict:
    key_of = jax.random.split(jax.random.key(seed), 4)
    part_keys = jax.random.split(jax.random.fold_in(key_of[3], part), 4)
    points = normal_values(part_keys[0], (F, N), 1.0, 6.0, ((1, 8),), jnp.float32)
    rhs = normal_values(part_keys[1], (R, N), 1.0, 6.0, ((1, 8),), jnp.float32)
    scales = jnp.clip(jnp.exp(jax.random.uniform(part_keys[2], (F,), jnp.float32, math.log(1.0), math.log(4.0))), 1.0, 4.0)
    return {"points": points, "rhs": rhs, "scales": scales}


ROOT5 = math.sqrt(5.0)
NOISE = 0.1

def matern(row_points, col_points):
    row_norms = lax.optimization_barrier(jnp.sum(row_points * row_points, axis=0))
    col_norms = lax.optimization_barrier(jnp.sum(col_points * col_points, axis=0))
    products = jnp.dot(row_points.T, col_points, precision=lax.Precision.HIGHEST, preferred_element_type=jnp.float32)
    squared = jnp.maximum(row_norms[:, None] + col_norms[None, :] - 2.0 * products, 0.0)
    distance = jnp.sqrt(squared)
    return (1.0 + ROOT5 * distance + 5.0 / 3.0 * squared) * jnp.exp(-ROOT5 * distance)

def reference(points, rhs, scales):
    scaled = points / scales[:, None]
    blocks = scaled.reshape(F, BLOCKS, B).transpose(1, 0, 2)

    def row_block_product(row_points):
        kernel_tile = matern(row_points, scaled)
        return jnp.dot(rhs, kernel_tile.T, precision=lax.Precision.HIGHEST, preferred_element_type=jnp.float32)
    stacked = lax.map(row_block_product, blocks)
    product = stacked.transpose(1, 0, 2).reshape(R, BLOCKS * B)
    return product + NOISE * rhs
```

```python
import math

import jax
import jax.numpy as jnp
from jax import lax
from jax.experimental import pallas as pl
from jax.experimental.pallas import tpu as pltpu
from jax.sharding import PartitionSpec as P

NOISE = 0.1
LOG2E = math.log2(math.e)
LN2 = math.log(2.0)
POINT_FACTOR = math.sqrt(5.0) * LOG2E
RHS_FACTOR = LN2 * LN2 / 3.0
SHIFT = 1.5 * LOG2E
REST = 0.75 * LOG2E * LOG2E
STEP = 256
DEPTH = 64


def three_parts(values):
    high = values.astype(jnp.bfloat16).astype(jnp.float32)
    rest = values - high
    middle = rest.astype(jnp.bfloat16).astype(jnp.float32)
    return high, middle, rest - middle


def factors(points, left):
    norms = jnp.sum(points * points, axis=0, keepdims=True)
    high, middle, low = three_parts(-2.0 * points if left else points)
    ones = [jnp.ones_like(norms)] * 3
    rows = [*three_parts(norms), *ones] if left else [*ones, *three_parts(norms)]
    rows.append(jnp.zeros((DEPTH - 54, points.shape[1]), jnp.float32))
    order = [high, high, middle, high, low, middle] if left else [high, middle, high, low, high, middle]
    return jnp.concatenate(order + rows, axis=0)


def multiply(a, b):
    return lax.dot_general(a, b, (((1,), (0,)), ((), ())), preferred_element_type=jnp.float32)


def tile_kernel(own_ref, other_ref, before_ref, out_ref, left_ref, total_ref):
    width = own_ref.shape[1]
    depth = other_ref.shape[1]
    right = factors(own_ref[:8], False).astype(jnp.bfloat16)
    left_ref[...] = factors(other_ref[:8], True).T.astype(jnp.bfloat16)
    values = other_ref[8:]
    high = values.astype(jnp.bfloat16).astype(jnp.float32)
    both = jnp.concatenate([high, values - high], axis=0).astype(jnp.bfloat16)
    single = jnp.concatenate([high, jnp.zeros_like(high)], axis=0).astype(jnp.bfloat16)
    total_ref[...] = jnp.zeros_like(total_ref)
    for j in range(0, depth, STEP):
        for i in range(0, width, STEP):
            squared = jnp.maximum(multiply(left_ref[j : j + STEP], right[:, i : i + STEP]), 1e-30)
            scaled = squared * lax.rsqrt(squared)
            shifted = scaled + SHIFT
            entries = (shifted * shifted + REST) * jnp.exp2(-scaled)
            rounded = entries.astype(jnp.bfloat16)
            remainder = (entries - rounded.astype(jnp.float32)).astype(jnp.bfloat16)
            total_ref[:, i : i + STEP] += multiply(both[:, j : j + STEP], rounded) + multiply(
                single[:, j : j + STEP], remainder
            )
    out_ref[...] = before_ref[...] + total_ref[:8] + total_ref[8:]


def tile(own, other, before):
    width, depth = own.shape[1], other.shape[1]
    in_vmem = pl.BlockSpec(memory_space=pltpu.VMEM)
    return pl.pallas_call(
        tile_kernel,
        out_shape=jax.ShapeDtypeStruct((8, width), jnp.float32),
        in_specs=[in_vmem] * 3,
        out_specs=in_vmem,
        scratch_shapes=[pltpu.VMEM((depth, DEPTH), jnp.bfloat16), pltpu.VMEM((16, width), jnp.float32)],
        compiler_params=pltpu.CompilerParams(vmem_limit_bytes=24 * 1024 * 1024),
        cost_estimate=pl.CostEstimate(
            flops=2 * 80 * width * depth, bytes_accessed=4 * 32 * depth, transcendentals=2 * width * depth
        ),
    )(own, other, before)


def local(points, rhs, scales):
    block_count = lax.axis_size("blk")
    section = lax.axis_index("section")
    half = block_count // 2
    mine = jnp.concatenate([points * (POINT_FACTOR / scales)[:, None], rhs * RHS_FACTOR], axis=0)
    others = []
    for step in range(half):
        pairs = [(2 * i + 1, 2 * (i ^ (half + step)) + 1) for i in range(block_count)]
        if step:
            pairs += [(2 * i, 2 * (i ^ step)) for i in range(block_count)]
        others.append(lax.ppermute(mine, ("blk", "section"), pairs))
    others[0] = jnp.where(section == 0, mine, others[0])
    total = jnp.zeros_like(rhs)
    for other in others:
        total = tile(mine, other, total)
    swapped = lax.ppermute(total, "section", [(0, 1), (1, 0)])
    return total + swapped + NOISE * rhs


def solution(mesh):
    in_specs = (P(None, ("parts", "blk")), P(None, ("parts", "blk")), P("parts"))
    out_specs = P(None, ("parts", "blk"))
    return jax.shard_map(local, mesh=mesh, in_specs=in_specs, out_specs=out_specs, check_vma=False)
```

```python
import math

import jax
import jax.numpy as jnp
from jax import lax
from jax.experimental import pallas as pl
from jax.experimental.pallas import tpu as pltpu
from jax.sharding import PartitionSpec as P

NOISE = 0.1
LOG2E = math.log2(math.e)
LN2 = math.log(2.0)
POINT_FACTOR = math.sqrt(5.0) * LOG2E
RHS_FACTOR = LN2 * LN2 / 3.0
SHIFT = 1.5 * LOG2E
REST = 0.75 * LOG2E * LOG2E
STEP = 256
DEPTH = 64
VMEM = pl.BlockSpec(memory_space=pltpu.VMEM)


def three_parts(values):
    high = values.astype(jnp.bfloat16).astype(jnp.float32)
    rest = values - high
    middle = rest.astype(jnp.bfloat16).astype(jnp.float32)
    return high, middle, rest - middle


def factors(points, left):
    norms = jnp.sum(points * points, axis=0, keepdims=True)
    high, middle, low = three_parts(-2.0 * points if left else points)
    ones = [jnp.ones_like(norms)] * 3
    rows = [*three_parts(norms), *ones] if left else [*ones, *three_parts(norms)]
    rows.append(jnp.zeros((DEPTH - 54, points.shape[1]), jnp.float32))
    order = [high, high, middle, high, low, middle] if left else [high, middle, high, low, high, middle]
    return jnp.concatenate(order + rows, axis=0)


def multiply(a, b):
    return lax.dot_general(a, b, (((1,), (0,)), ((), ())), preferred_element_type=jnp.float32)


def tile_kernel(count, rows_ref, *refs):
    columns, (before_ref, out_ref, left_ref, total_ref) = refs[:count], refs[count:]
    width = rows_ref.shape[1]
    depth = columns[0].shape[1]
    right = factors(rows_ref[:8] * POINT_FACTOR, False).astype(jnp.bfloat16)
    total_ref[...] = jnp.zeros_like(total_ref)
    for column in columns:
        left_ref[...] = factors(column[:8] * POINT_FACTOR, True).T.astype(jnp.bfloat16)
        values = column[8:] * RHS_FACTOR
        high = values.astype(jnp.bfloat16).astype(jnp.float32)
        both = jnp.concatenate([high, values - high], axis=0).astype(jnp.bfloat16)
        single = jnp.concatenate([high, jnp.zeros_like(high)], axis=0).astype(jnp.bfloat16)
        for j in range(0, depth, STEP):
            for i in range(0, width, STEP):
                squared = jnp.maximum(multiply(left_ref[j : j + STEP], right[:, i : i + STEP]), 1e-30)
                scaled = squared * lax.rsqrt(squared)
                shifted = scaled + SHIFT
                entries = (shifted * shifted + REST) * jnp.exp2(-scaled)
                rounded = entries.astype(jnp.bfloat16)
                remainder = (entries - rounded.astype(jnp.float32)).astype(jnp.bfloat16)
                total_ref[:, i : i + STEP] += multiply(both[:, j : j + STEP], rounded) + multiply(
                    single[:, j : j + STEP], remainder
                )
    out_ref[...] = before_ref[...] + total_ref[:8] + total_ref[8:]


def tiles(rows, columns, before):
    width, depth = rows.shape[1], columns[0].shape[1]
    entries = width * depth * len(columns)
    return pl.pallas_call(
        lambda *refs: tile_kernel(len(columns), *refs),
        out_shape=jax.ShapeDtypeStruct((8, width), jnp.float32),
        in_specs=[VMEM] * (len(columns) + 2),
        out_specs=VMEM,
        scratch_shapes=[pltpu.VMEM((depth, DEPTH), jnp.bfloat16), pltpu.VMEM((16, width), jnp.float32)],
        compiler_params=pltpu.CompilerParams(vmem_limit_bytes=24 * 1024 * 1024),
        cost_estimate=pl.CostEstimate(flops=160 * entries, bytes_accessed=4 * 32 * depth, transcendentals=2 * entries),
    )(rows, *columns, before)


def local(points, rhs, scales):
    block_count = lax.axis_size("blk")
    mine = jnp.concatenate([points / scales[:, None], rhs], axis=0)
    rows = mine[:8]

    def fetch(array, offsets):
        pairs = [(2 * i + s, 2 * (i ^ k) + s) for s, k in enumerate(offsets) if k for i in range(block_count)]
        return lax.ppermute(array, ("blk", "section"), pairs)

    partner_rows = fetch(rows, (1, 1))
    columns = [fetch(mine, (offset, offset + 2)) for offset in range(0, block_count, 4)]
    columns[0] = jnp.where(lax.axis_index("section") == 0, mine, columns[0])
    zeros = jnp.zeros_like(rhs)
    first = tiles(rows, columns[:1], zeros)
    first, again = lax.optimization_barrier((first, zeros))
    for_partner = tiles(partner_rows, columns, again)
    returned = fetch(for_partner, (1, 1))
    total = tiles(rows, columns[1:], first) + returned
    swapped = lax.ppermute(total, "section", [(0, 1), (1, 0)])
    return total + swapped + NOISE * rhs


def solution(mesh):
    in_specs = (P(None, ("parts", "blk")), P(None, ("parts", "blk")), P("parts"))
    out_specs = P(None, ("parts", "blk"))
    return jax.shard_map(local, mesh=mesh, in_specs=in_specs, out_specs=out_specs, check_vma=False)
```

```python
import math

import jax
import jax.numpy as jnp
from jax import lax
from jax.experimental import pallas as pl
from jax.experimental.pallas import tpu as pltpu
from jax.sharding import PartitionSpec as P

NOISE = 0.1
POINT_FACTOR = math.sqrt(5.0) / 3.0
RHS_FACTOR = 3.0
DECAY = -3.0 * math.log2(math.e)
STEP = 256
DEPTH = 64
VMEM = pl.BlockSpec(memory_space=pltpu.VMEM)


def three_parts(values):
    high = values.astype(jnp.bfloat16).astype(jnp.float32)
    rest = values - high
    middle = rest.astype(jnp.bfloat16).astype(jnp.float32)
    return high, middle, rest - middle


def factors(points, left):
    norms = jnp.sum(points * points, axis=0, keepdims=True)
    high, middle, low = three_parts(-2.0 * points if left else points)
    ones = [jnp.ones_like(norms)] * 3
    rows = [*three_parts(norms), *ones] if left else [*ones, *three_parts(norms)]
    rows.append(jnp.zeros((DEPTH - 54, points.shape[1]), jnp.float32))
    order = [high, high, middle, high, low, middle] if left else [high, middle, high, low, high, middle]
    return jnp.concatenate(order + rows, axis=0)


def multiply(a, b):
    return lax.dot_general(a, b, (((1,), (0,)), ((), ())), preferred_element_type=jnp.float32)


def tile_kernel(known, made, *refs):
    rows_ref, refs = refs[0], refs[1:]
    columns, refs = refs[: known + made], refs[known + made :]
    lefts, refs = refs[:known], refs[known:]
    before_ref, out_ref, refs = refs[0], refs[1], refs[2:]
    lefts, refs = [*lefts, *refs[:made]], refs[made:]
    total_ref = refs[-1]
    right_ref = rows_ref
    if rows_ref.dtype == jnp.float32:
        right_ref = refs[0]
        right_ref[...] = factors(rows_ref[:8] * POINT_FACTOR, False).astype(jnp.bfloat16)
    total_ref[...] = jnp.zeros_like(total_ref)
    for n, (column, left_ref) in enumerate(zip(columns, lefts)):
        if n >= known:
            left_ref[...] = factors(column[:8] * POINT_FACTOR, True).T.astype(jnp.bfloat16)
        values = column[8:] * RHS_FACTOR
        high = values.astype(jnp.bfloat16).astype(jnp.float32)
        both = jnp.concatenate([high, values - high], axis=0).astype(jnp.bfloat16)
        single = jnp.concatenate([high, jnp.zeros_like(high)], axis=0).astype(jnp.bfloat16)
        for j in range(0, column.shape[1], STEP):
            for i in range(0, right_ref.shape[1], STEP):
                product = multiply(left_ref[j : j + STEP], right_ref[:, i : i + STEP])
                squared = jnp.maximum(product, 1e-30)
                scaled = squared * lax.rsqrt(squared)
                entries = (squared + (scaled + 1.0 / 3.0)) * jnp.exp2(scaled * DECAY)
                rounded = entries.astype(jnp.bfloat16)
                remainder = (entries - rounded.astype(jnp.float32)).astype(jnp.bfloat16)
                total_ref[:, i : i + STEP] += multiply(both[:, j : j + STEP], rounded) + multiply(
                    single[:, j : j + STEP], remainder
                )
    out_ref[...] = before_ref[...] + total_ref[:8] + total_ref[8:]


def tiles(rows, columns, lefts, before):
    width, depth = rows.shape[1], columns[0].shape[1]
    known, made = len(lefts), len(columns) - len(lefts)
    fresh = rows.dtype == jnp.float32
    entries = width * depth * len(columns)
    out, *new = pl.pallas_call(
        lambda *refs: tile_kernel(known, made, *refs),
        out_shape=[jax.ShapeDtypeStruct((8, width), jnp.float32)]
        + [jax.ShapeDtypeStruct((depth, DEPTH), jnp.bfloat16)] * made
        + [jax.ShapeDtypeStruct((DEPTH, width), jnp.bfloat16)] * fresh,
        in_specs=[VMEM] * (2 + known + len(columns)),
        out_specs=[VMEM] * (1 + made + fresh),
        scratch_shapes=[pltpu.VMEM((16, width), jnp.float32)],
        compiler_params=pltpu.CompilerParams(vmem_limit_bytes=24 * 1024 * 1024),
        cost_estimate=pl.CostEstimate(flops=160 * entries, bytes_accessed=4 * 32 * depth, transcendentals=2 * entries),
    )(rows, *columns, *lefts, before)
    return out, new.pop() if fresh else rows, [*lefts, *new]


def local(points, rhs, scales):
    block_count = lax.axis_size("blk")
    mine = jnp.concatenate([points / scales[:, None], rhs], axis=0)

    def fetch(array, offsets):
        pairs = [(2 * i + s, 2 * (i ^ k) + s) for s, k in enumerate(offsets) if k for i in range(block_count)]
        return lax.ppermute(array, ("blk", "section"), pairs)

    partner_rows = fetch(mine, (1, 1))
    columns = [fetch(mine, (offset, offset + 2)) for offset in range(0, block_count, 4)]
    columns[0] = jnp.where(lax.axis_index("section") == 0, mine, columns[0])
    zeros = jnp.zeros_like(rhs)
    first, right, lefts = tiles(mine[:8], columns[:1], [], zeros)
    first, again = lax.optimization_barrier((first, zeros))
    for_partner, _, lefts = tiles(partner_rows[:8], columns, lefts, again)
    returned = fetch(for_partner, (1, 1))
    total, _, _ = tiles(right, columns[1:], lefts[1:], first)
    total = total + returned
    swapped = lax.ppermute(total, "section", [(0, 1), (1, 0)])
    return total + swapped + NOISE * rhs


def solution(mesh):
    in_specs = (P(None, ("parts", "blk")), P(None, ("parts", "blk")), P("parts"))
    out_specs = P(None, ("parts", "blk"))
    return jax.shard_map(local, mesh=mesh, in_specs=in_specs, out_specs=out_specs, check_vma=False)
```

```python
import math

import jax
import jax.numpy as jnp
from jax import lax
from jax.experimental import pallas as pl
from jax.experimental.pallas import tpu as pltpu
from jax.sharding import PartitionSpec as P

NOISE = 0.1
POINT_FACTOR = math.sqrt(5.0) / 3.0
RHS_FACTOR = 3.0
DECAY = -3.0 * math.log2(math.e)
STEP = 256
DEPTH = 64
VMEM = pl.BlockSpec(memory_space=pltpu.VMEM)


def three_parts(values):
    high = values.astype(jnp.bfloat16).astype(jnp.float32)
    rest = values - high
    middle = rest.astype(jnp.bfloat16).astype(jnp.float32)
    return high, middle, rest - middle


def factors(points, left):
    norms = jnp.sum(points * points, axis=0, keepdims=True)
    high, middle, low = three_parts(-2.0 * points if left else points)
    ones = [jnp.ones_like(norms)] * 3
    rows = [*three_parts(norms), *ones] if left else [*ones, *three_parts(norms)]
    rows.append(jnp.zeros((DEPTH - 54, points.shape[1]), jnp.float32))
    order = [high, high, middle, high, low, middle] if left else [high, middle, high, low, high, middle]
    return jnp.concatenate(order + rows, axis=0)


def multiply(a, b):
    return lax.dot_general(a, b, (((1,), (0,)), ((), ())), preferred_element_type=jnp.float32)


def tile_kernel(known, made, *refs):
    rows_ref, refs = refs[0], refs[1:]
    columns, refs = refs[: known + made], refs[known + made :]
    lefts, refs = refs[:known], refs[known:]
    before_ref, out_ref, refs = refs[0], refs[1], refs[2:]
    lefts, refs = [*lefts, *refs[:made]], refs[made:]
    total_ref = refs[-1]
    right_ref = rows_ref
    if rows_ref.dtype == jnp.float32:
        right_ref = refs[0]
        right_ref[...] = factors(rows_ref[:8] * POINT_FACTOR, False).astype(jnp.bfloat16)
    total_ref[...] = jnp.zeros_like(total_ref)
    for n, (column, left_ref) in enumerate(zip(columns, lefts)):
        if n >= known:
            left_ref[...] = factors(column[:8] * POINT_FACTOR, True).T.astype(jnp.bfloat16)
        values = column[8:] * RHS_FACTOR
        high = values.astype(jnp.bfloat16).astype(jnp.float32)
        both = jnp.concatenate([high, values - high], axis=0).astype(jnp.bfloat16)
        single = jnp.concatenate([high, jnp.zeros_like(high)], axis=0).astype(jnp.bfloat16)
        for j in range(0, column.shape[1], STEP):
            for i in range(0, right_ref.shape[1], STEP):
                product = multiply(left_ref[j : j + STEP], right_ref[:, i : i + STEP])
                squared = jnp.maximum(product, 1e-30)
                scaled = squared * lax.rsqrt(squared)
                entries = (squared + (scaled + 1.0 / 3.0)) * jnp.exp2(scaled * DECAY)
                rounded = entries.astype(jnp.bfloat16)
                remainder = (entries - rounded.astype(jnp.float32)).astype(jnp.bfloat16)
                total_ref[:, i : i + STEP] += multiply(both[:, j : j + STEP], rounded) + multiply(
                    single[:, j : j + STEP], remainder
                )
    out_ref[...] = before_ref[...] + total_ref[:8] + total_ref[8:]


def tiles(rows, columns, lefts, before):
    width, depth = rows.shape[1], columns[0].shape[1]
    known, made = len(lefts), len(columns) - len(lefts)
    fresh = rows.dtype == jnp.float32
    entries = width * depth * len(columns)
    out, *new = pl.pallas_call(
        lambda *refs: tile_kernel(known, made, *refs),
        out_shape=[jax.ShapeDtypeStruct((8, width), jnp.float32)]
        + [jax.ShapeDtypeStruct((depth, DEPTH), jnp.bfloat16)] * made
        + [jax.ShapeDtypeStruct((DEPTH, width), jnp.bfloat16)] * fresh,
        in_specs=[VMEM] * (2 + known + len(columns)),
        out_specs=[VMEM] * (1 + made + fresh),
        scratch_shapes=[pltpu.VMEM((16, width), jnp.float32)],
        compiler_params=pltpu.CompilerParams(vmem_limit_bytes=24 * 1024 * 1024),
        cost_estimate=pl.CostEstimate(flops=160 * entries, bytes_accessed=4 * 32 * depth, transcendentals=2 * entries),
    )(rows, *columns, *lefts, before)
    return out, new.pop() if fresh else rows, [*lefts, *new]


def local(points, rhs, scales):
    block_count = lax.axis_size("blk")
    mine = jnp.concatenate([points / scales[:, None], rhs], axis=0)

    def fetch(array, offsets):
        pairs = [(2 * i + s, 2 * (i ^ k) + s) for s, k in enumerate(offsets) for i in range(block_count)]
        return lax.ppermute(array, ("blk", "section"), pairs)

    def swap(array):
        return lax.ppermute(array, "section", [(0, 1), (1, 0)])

    first_section = lax.axis_index("section") == 0
    offsets = [1, *range(2, block_count, 2)]
    half = block_count // 4
    columns = [fetch(mine, pair) for pair in zip(offsets[:half], offsets[half:])]
    given_rows = swap(columns[0][:8])
    zeros = jnp.zeros_like(rhs)
    first, right, lefts = tiles(mine[:8], columns[:1], [], zeros)
    first, again, *columns[1:] = lax.optimization_barrier((first, zeros, *columns[1:]))
    partner_rows = jnp.where(first_section, columns[0][:8], given_rows)
    for_partner, _, lefts = tiles(partner_rows, columns, lefts, again)
    returned = fetch(for_partner, (1, 1))
    total, _, _ = tiles(right, columns[1:], lefts[1:], first)
    total = total + returned
    return total + swap(total) + NOISE * rhs


def solution(mesh):
    in_specs = (P(None, ("parts", "blk")), P(None, ("parts", "blk")), P("parts"))
    out_specs = P(None, ("parts", "blk"))
    return jax.shard_map(local, mesh=mesh, in_specs=in_specs, out_specs=out_specs, check_vma=False)
```

```python
import math

import jax
import jax.numpy as jnp
from jax import lax
from jax.experimental import pallas as pl
from jax.experimental.pallas import tpu as pltpu
from jax.sharding import PartitionSpec as P

NOISE = 0.1
POINT_FACTOR = math.sqrt(5.0) / 3.0
RHS_FACTOR = 3.0
DECAY = -3.0 * math.log2(math.e)
STEP = 256
DEPTH = 64
VMEM = pl.BlockSpec(memory_space=pltpu.VMEM)


def three_parts(values):
    high = values.astype(jnp.bfloat16).astype(jnp.float32)
    rest = values - high
    middle = rest.astype(jnp.bfloat16).astype(jnp.float32)
    return high, middle, rest - middle


def factors(points, left):
    high, middle, low = three_parts(-2.0 * points if left else points)
    kept = -0.5 * high if left else high
    norms = [jnp.sum(kept * kept, axis=0, keepdims=True), jnp.sum((points - kept) * (points + kept), axis=0, keepdims=True)]
    norms = [part for norm in norms for part in three_parts(norm)]
    ones = [jnp.ones_like(norms[0])] * len(norms)
    rows = norms + ones if left else ones + norms
    rows.append(jnp.zeros((DEPTH - 60, points.shape[1]), jnp.float32))
    order = [high, high, middle, high, low, middle] if left else [high, middle, high, low, high, middle]
    return jnp.concatenate(order + rows, axis=0)


def multiply(a, b):
    return lax.dot_general(a, b, (((1,), (0,)), ((), ())), preferred_element_type=jnp.float32)


def tile_kernel(known, made, *refs):
    rows_ref, refs = refs[0], refs[1:]
    columns, refs = refs[: known + made], refs[known + made :]
    lefts, refs = refs[:known], refs[known:]
    before_ref, out_ref, refs = refs[0], refs[1], refs[2:]
    lefts, refs = [*lefts, *refs[:made]], refs[made:]
    total_ref = refs[-1]
    right_ref = rows_ref
    if rows_ref.dtype == jnp.float32:
        right_ref = refs[0]
        right_ref[...] = factors(rows_ref[:8] * POINT_FACTOR, False).astype(jnp.bfloat16)
    total_ref[...] = jnp.zeros_like(total_ref)
    for n, (column, left_ref) in enumerate(zip(columns, lefts)):
        if n >= known:
            left_ref[...] = factors(column[:8] * POINT_FACTOR, True).T.astype(jnp.bfloat16)
        values = column[8:] * RHS_FACTOR
        high = values.astype(jnp.bfloat16).astype(jnp.float32)
        both = jnp.concatenate([high, values - high], axis=0).astype(jnp.bfloat16)
        single = jnp.concatenate([high, jnp.zeros_like(high)], axis=0).astype(jnp.bfloat16)
        for j in range(0, column.shape[1], STEP):
            for i in range(0, right_ref.shape[1], STEP):
                product = multiply(left_ref[j : j + STEP], right_ref[:, i : i + STEP])
                squared = jnp.maximum(product, 1e-30)
                scaled = squared * lax.rsqrt(squared)
                entries = (squared + (scaled + 1.0 / 3.0)) * jnp.exp2(scaled * DECAY)
                rounded = entries.astype(jnp.bfloat16)
                remainder = (entries - rounded.astype(jnp.float32)).astype(jnp.bfloat16)
                total_ref[:, i : i + STEP] += multiply(both[:, j : j + STEP], rounded) + multiply(
                    single[:, j : j + STEP], remainder
                )
    out_ref[...] = before_ref[...] + total_ref[:8] + total_ref[8:]


def tiles(rows, columns, lefts, before):
    width, depth = rows.shape[1], columns[0].shape[1]
    known, made = len(lefts), len(columns) - len(lefts)
    fresh = rows.dtype == jnp.float32
    entries = width * depth * len(columns)
    out, *new = pl.pallas_call(
        lambda *refs: tile_kernel(known, made, *refs),
        out_shape=[jax.ShapeDtypeStruct((8, width), jnp.float32)]
        + [jax.ShapeDtypeStruct((depth, DEPTH), jnp.bfloat16)] * made
        + [jax.ShapeDtypeStruct((DEPTH, width), jnp.bfloat16)] * fresh,
        in_specs=[VMEM] * (2 + known + len(columns)),
        out_specs=[VMEM] * (1 + made + fresh),
        scratch_shapes=[pltpu.VMEM((16, width), jnp.float32)],
        compiler_params=pltpu.CompilerParams(vmem_limit_bytes=24 * 1024 * 1024),
        cost_estimate=pl.CostEstimate(flops=160 * entries, bytes_accessed=4 * 32 * depth, transcendentals=2 * entries),
    )(rows, *columns, *lefts, before)
    return out, new.pop() if fresh else rows, [*lefts, *new]


def local(points, rhs, scales):
    block_count = lax.axis_size("blk")
    mine = jnp.concatenate([points / scales[:, None], rhs], axis=0)

    def fetch(array, offsets):
        pairs = [(2 * i + s, 2 * (i ^ k) + s) for s, k in enumerate(offsets) for i in range(block_count)]
        return lax.ppermute(array, ("blk", "section"), pairs)

    def swap(array):
        return lax.ppermute(array, "section", [(0, 1), (1, 0)])

    first_section = lax.axis_index("section") == 0
    offsets = [1, *range(2, block_count, 2)]
    half = block_count // 4
    columns = [fetch(mine, pair) for pair in zip(offsets[:half], offsets[half:])]
    given_rows = swap(columns[0][:8])
    zeros = jnp.zeros_like(rhs)
    first, right, lefts = tiles(mine[:8], columns[:1], [], zeros)
    first, again, *columns[1:] = lax.optimization_barrier((first, zeros, *columns[1:]))
    partner_rows = jnp.where(first_section, columns[0][:8], given_rows)
    for_partner, _, lefts = tiles(partner_rows, columns, lefts, again)
    returned = fetch(for_partner, (1, 1))
    total, _, _ = tiles(right, columns[1:], lefts[1:], first)
    total = total + returned
    return total + swap(total) + NOISE * rhs


def solution(mesh):
    in_specs = (P(None, ("parts", "blk")), P(None, ("parts", "blk")), P("parts"))
    out_specs = P(None, ("parts", "blk"))
    return jax.shard_map(local, mesh=mesh, in_specs=in_specs, out_specs=out_specs, check_vma=False)
```

```python
import math

import jax
import jax.numpy as jnp
from jax import lax
from jax.experimental import pallas as pl
from jax.experimental.pallas import tpu as pltpu
from jax.sharding import PartitionSpec as P

NOISE = 0.1
POINT_FACTOR = math.sqrt(5.0) / 3.0
RHS_FACTOR = 3.0
DECAY = -3.0 * math.log2(math.e)
STEP = 256
DEPTH = 64
VMEM = pl.BlockSpec(memory_space=pltpu.VMEM)


def three_parts(values):
    high = values.astype(jnp.bfloat16).astype(jnp.float32)
    rest = values - high
    middle = rest.astype(jnp.bfloat16).astype(jnp.float32)
    return high, middle, rest - middle


def factors(points, left):
    high, middle, low = three_parts(-2.0 * points if left else points)
    kept = -0.5 * high if left else high
    norms = [jnp.sum(kept * kept, axis=0, keepdims=True), jnp.sum((points - kept) * (points + kept), axis=0, keepdims=True)]
    norms = [part for norm in norms for part in three_parts(norm)]
    ones = [jnp.ones_like(norms[0])] * len(norms)
    rows = norms + ones if left else ones + norms
    rows.append(jnp.zeros((DEPTH - 60, points.shape[1]), jnp.float32))
    order = [high, high, middle, high, low, middle] if left else [high, middle, high, low, high, middle]
    return jnp.concatenate(order + rows, axis=0)


def multiply(a, b):
    return lax.dot_general(a, b, (((1,), (0,)), ((), ())), preferred_element_type=jnp.float32)


def tile_kernel(known, made, *refs):
    rows_ref, refs = refs[0], refs[1:]
    columns, refs = refs[: known + made], refs[known + made :]
    lefts, refs = refs[:known], refs[known:]
    before_ref, out_ref, refs = refs[0], refs[1], refs[2:]
    lefts, refs = [*lefts, *refs[:made]], refs[made:]
    total_ref = refs[-1]
    right_ref = rows_ref
    if rows_ref.dtype == jnp.float32:
        right_ref = refs[0]
        right_ref[...] = factors(rows_ref[:8] * POINT_FACTOR, False).astype(jnp.bfloat16)
    total_ref[...] = jnp.zeros_like(total_ref)
    for n, (column, left_ref) in enumerate(zip(columns, lefts)):
        if n >= known:
            left_ref[...] = factors(column[:8] * POINT_FACTOR, True).T.astype(jnp.bfloat16)
        values = column[8:] * RHS_FACTOR
        high = values.astype(jnp.bfloat16).astype(jnp.float32)
        both = jnp.concatenate([high, values - high], axis=0).astype(jnp.bfloat16)
        single = jnp.concatenate([high, jnp.zeros_like(high)], axis=0).astype(jnp.bfloat16)
        for i in range(0, right_ref.shape[1], STEP):
            for j in range(0, column.shape[1], STEP):
                product = multiply(left_ref[j : j + STEP], right_ref[:, i : i + STEP])
                squared = jnp.maximum(product, 1e-30)
                scaled = squared * lax.rsqrt(squared)
                entries = (squared + (scaled + 1.0 / 3.0)) * jnp.exp2(scaled * DECAY)
                rounded = entries.astype(jnp.bfloat16)
                remainder = (entries - rounded.astype(jnp.float32)).astype(jnp.bfloat16)
                total_ref[:, i : i + STEP] += multiply(both[:, j : j + STEP], rounded) + multiply(
                    single[:, j : j + STEP], remainder
                )
    out_ref[...] = before_ref[...] + total_ref[:8] + total_ref[8:]


def tiles(rows, columns, lefts, before):
    width, depth = rows.shape[1], columns[0].shape[1]
    known, made = len(lefts), len(columns) - len(lefts)
    fresh = rows.dtype == jnp.float32
    entries = width * depth * len(columns)
    out, *new = pl.pallas_call(
        lambda *refs: tile_kernel(known, made, *refs),
        out_shape=[jax.ShapeDtypeStruct((8, width), jnp.float32)]
        + [jax.ShapeDtypeStruct((depth, DEPTH), jnp.bfloat16)] * made
        + [jax.ShapeDtypeStruct((DEPTH, width), jnp.bfloat16)] * fresh,
        in_specs=[VMEM] * (2 + known + len(columns)),
        out_specs=[VMEM] * (1 + made + fresh),
        scratch_shapes=[pltpu.VMEM((16, width), jnp.float32)],
        compiler_params=pltpu.CompilerParams(vmem_limit_bytes=24 * 1024 * 1024),
        cost_estimate=pl.CostEstimate(flops=160 * entries, bytes_accessed=4 * 32 * depth, transcendentals=2 * entries),
    )(rows, *columns, *lefts, before)
    return out, new.pop() if fresh else rows, [*lefts, *new]


def local(points, rhs, scales):
    block_count = lax.axis_size("blk")
    mine = jnp.concatenate([points / scales[:, None], rhs], axis=0)

    def fetch(array, offsets):
        pairs = [(2 * i + s, 2 * (i ^ k) + s) for s, k in enumerate(offsets) for i in range(block_count)]
        return lax.ppermute(array, ("blk", "section"), pairs)

    def swap(array):
        return lax.ppermute(array, "section", [(0, 1), (1, 0)])

    first_section = lax.axis_index("section") == 0
    offsets = [1, *range(2, block_count, 2)]
    half = block_count // 4
    columns = [fetch(mine, pair) for pair in zip(offsets[:half], offsets[half:])]
    given_rows = swap(columns[0][:8])
    zeros = jnp.zeros_like(rhs)
    first, right, lefts = tiles(mine[:8], columns[:1], [], zeros)
    first, again, *columns[1:] = lax.optimization_barrier((first, zeros, *columns[1:]))
    partner_rows = jnp.where(first_section, columns[0][:8], given_rows)
    for_partner, _, lefts = tiles(partner_rows, columns, lefts, again)
    returned = fetch(for_partner, (1, 1))
    total, _, _ = tiles(right, columns[1:], lefts[1:], first)
    total = total + returned
    return total + swap(total) + NOISE * rhs


def solution(mesh):
    in_specs = (P(None, ("parts", "blk")), P(None, ("parts", "blk")), P("parts"))
    out_specs = P(None, ("parts", "blk"))
    return jax.shard_map(local, mesh=mesh, in_specs=in_specs, out_specs=out_specs, check_vma=False)
```
